512 devices in a mesh: dp: 4 (over y), group: 16 (over x, z_hi), tensor: 8 (over z_lo, core).
Axes of the slice: x: 4, y: 4, z: 16 (z_hi: 4, z_lo: 4; z = z_hi * 4 + z_lo), core: 2. Of those that a mesh axis runs over, the one named last changes fastest.
Arguments:
- queries: bfloat16 [64, 128, 8192], P(('dp', 'group'), None, 'tensor'), parts along dimension 0, may hold values from -9 to 9
- comp_keys: bfloat16 [64, 128, 1024], P(('dp', 'group'), None, 'tensor'), parts along dimension 0, may hold values from -4 to 4
- comp_values: bfloat16 [64, 128, 1024], P(('dp', 'group'), None, 'tensor'), parts along dimension 0, may hold values from -6 to 6
- prompt_keys: bfloat16 [8192, 1024], P(('dp', 'group'), 'tensor'), parts along dimension 0, may hold values from -9 to 9
- prompt_values: bfloat16 [8192, 1024], P(('dp', 'group'), 'tensor'), parts along dimension 0, may hold values from -6 to 6
- out_grad: bfloat16 [64, 128, 8192], P(('dp', 'group'), None, 'tensor'), parts along dimension 0, may hold values from -192 to 192
- lengths: int32 [64], P(('dp', 'group')), parts along dimension 0, may hold values from 1 to 128
- loss_mask: int32 [64, 128], P(('dp', 'group')), parts along dimension 0, may hold values 0 or 1
- buckets: int32 [64], P(('dp', 'group')), parts along dimension 0, may hold values from 0 to 10
Outputs:
- query_grad: float32 [64, 128, 8192], P(('dp', 'group'), None, 'tensor'), parts along dimension 0
- comp_key_grad: float32 [64, 128, 1024], P(('dp', 'group'), None, 'tensor'), parts along dimension 0
- comp_value_grad: float32 [64, 128, 1024], P(('dp', 'group'), None, 'tensor'), parts along dimension 0
- prompt_key_grad: float32 [8192, 1024], P(('dp', 'group'), 'tensor'), parts along dimension 0
- prompt_value_grad: float32 [8192, 1024], P(('dp', 'group'), 'tensor'), parts along dimension 0
The draws below stay inside these ranges and needn't reach their ends.
There are 4 independent parts, one for each index of `dp`. The reference program is written for one: setup_inputs(seed, part) draws one part's arguments, and reference() takes and returns one part's arrays. A program takes and returns all parts, laid end to end along the dimension named above; each array names one. Nothing has to cross between parts.
All inputs are finite; a program needn't handle non-finite values. No bound on the sum of `loss_mask` on one device may be relied on, other than what follows from the above.
Results may differ from the reference program's by a relative error of at most 0.025.
Values may be sent and summed in bfloat16 or wider, within the bound.
No kernel may reach another device: no remote copies, remote signals or barrier semaphores. Data moves between devices by JAX's collectives and lax.ppermute only.
A program may use at most 64 MiB of HBM per device.

```python
import jax
import jax.numpy as jnp
from jax import lax

HEADS = 64
KV_HEADS = 8
HEAD_DIM = 128
COMP_LEN = 128
REWARD_LEVELS = 11
COMPLETIONS = 16
PROMPT = 2048


def draw_queries(key, part):
    key = jax.random.fold_in(key, 11)
    full_shape = (COMPLETIONS, COMP_LEN, HEADS * HEAD_DIM)
    result = jax.random.truncated_normal(key, -4.0, 4.0, full_shape, jnp.float32)
    return result.astype(jnp.bfloat16)


def draw_prompt_keys(key, part):
    key = jax.random.fold_in(key, 17)
    full_shape = (PROMPT, KV_HEADS * HEAD_DIM)
    result = jax.random.truncated_normal(key, -4.0, 4.0, full_shape, jnp.float32)
    return result.astype(jnp.bfloat16)


def draw_lengths(key, part):
    key = jax.random.fold_in(key, 3)
    comp_index = jnp.arange(COMPLETIONS, dtype=jnp.int32)
    base_length = COMP_LEN // 3 + (COMP_LEN - COMP_LEN // 3) * comp_index // max(COMPLETIONS - 1, 1)
    spread = max(COMP_LEN // 8, 1)
    jitter_values = jax.random.randint(key, (COMPLETIONS,), -spread, spread + 1)
    drawn = jnp.clip(base_length + jitter_values, 1, COMP_LEN)
    return jnp.where(comp_index == COMPLETIONS - 1, COMP_LEN, drawn).astype(jnp.int32)


def with_ends(values, key, low, high):
    longest = values.shape.index(max(values.shape))
    spots = []
    for shift in (0, 1):
        where = [jax.random.randint(jax.random.fold_in(key, axis), (), 0, length) for axis, length in enumerate(values.shape)]
        where[longest] = (where[longest] + shift) % values.shape[longest]
        spots.append(tuple(where))
    return values.at[spots[0]].set(low).at[spots[1]].set(high)


def level_of(key, shape, shards, smallest, largest):
    factor_of = 1.0
    for position, parts in shards:
        steps = jax.random.uniform(jax.random.fold_in(jax.random.fold_in(key, 6), position), (parts,), jnp.float32, smallest / len(shards), largest / len(shards))
        factor_of = factor_of * jnp.repeat(jnp.exp(steps), shape[position] // parts).reshape((-1,) + (1,) * (len(shape) - 1 - position))
    return factor_of


def bell_draw(stream_key, extent, deviation, most, pieces=(), kind=jnp.bfloat16):
    values = jax.random.normal(stream_key, extent, jnp.float32) * deviation
    if len(pieces) > 0:
        values = level_of(stream_key, extent, pieces, -0.22, 0.18) * values
    return jnp.clip(values, min=-most, max=most).astype(kind)


def setup_inputs(seed: int = 0, part: int = 0) -> dict:
    arg_keys = jax.random.split(jax.random.key(seed), 10)
    part_splits = jax.random.split(jax.random.fold_in(arg_keys[9], part), 10)
    return {
        "queries": draw_queries(jax.random.fold_in(jax.random.fold_in(arg_keys[9], part), 71), part),
        "comp_keys": bell_draw(part_splits[1], (COMPLETIONS, COMP_LEN, KV_HEADS * HEAD_DIM), 1.0, 4.0, ((0, 16), (2, 8))),
        "comp_values": bell_draw(part_splits[2], (COMPLETIONS, COMP_LEN, KV_HEADS * HEAD_DIM), 1.0, 6.0, ((0, 16), (2, 8))),
        "prompt_keys": draw_prompt_keys(jax.random.fold_in(jax.random.fold_in(arg_keys[9], part), 71), part),
        "prompt_values": bell_draw(part_splits[4], (PROMPT, KV_HEADS * HEAD_DIM), 1.0, 6.0, ((0, 16), (1, 8))),
        "out_grad": bell_draw(part_splits[5], (COMPLETIONS, COMP_LEN, HEADS * HEAD_DIM), 32.0, 192.0, ((0, 16), (2, 8))),
        "lengths": draw_lengths(jax.random.fold_in(jax.random.fold_in(arg_keys[9], part), 71), part),
        "loss_mask": with_ends((jax.random.randint(part_splits[7], (COMPLETIONS, COMP_LEN), 0, 4) < 3).astype(jnp.int32), jax.random.fold_in(part_splits[7], 1), 0, 1),
        "buckets": with_ends(jax.random.randint(part_splits[8], (COMPLETIONS,), 0, REWARD_LEVELS), jax.random.fold_in(part_splits[8], 1), 0, REWARD_LEVELS - 1).astype(jnp.int32),
    }


def token_weights(lengths, loss_mask, buckets):
    completions = lengths.shape[0]
    comp_len = loss_mask.shape[1]
    positions = jnp.arange(comp_len, dtype=jnp.int32)
    within = (positions[None, :] < lengths[:, None]).astype(jnp.int32)
    valid_tokens = (loss_mask * within).astype(jnp.float32)
    length_sum = jnp.sum(lengths.astype(jnp.float32))
    rewards = buckets.astype(jnp.float32)
    reward_mean = jnp.sum(rewards) / completions
    variance = jnp.sum(rewards * rewards) / completions - reward_mean * reward_mean
    advantage = (rewards - reward_mean) / jnp.sqrt(variance + 1.0)
    return advantage[:, None] * valid_tokens * (completions * comp_len / length_sum)

def attend_one(query_rows, own_key, own_value, grad_rows, prompt_keys, prompt_values):
    comp_len = query_rows.shape[0]
    score_scale = HEAD_DIM ** (-0.5)
    head_ratio = HEADS // KV_HEADS
    kv_width = KV_HEADS * HEAD_DIM
    all_keys = jnp.concatenate([prompt_keys, own_key], 0).astype(jnp.float32).reshape(-1, KV_HEADS, HEAD_DIM)
    all_values = jnp.concatenate([prompt_values, own_value], 0).astype(jnp.float32).reshape(-1, KV_HEADS, HEAD_DIM)
    query_heads = query_rows.astype(jnp.float32).reshape(comp_len, KV_HEADS, head_ratio, HEAD_DIM).transpose(1, 2, 0, 3)
    grad_heads = grad_rows.astype(jnp.float32).reshape(comp_len, KV_HEADS, head_ratio, HEAD_DIM).transpose(1, 2, 0, 3)
    scores = jnp.einsum('grtd,ngd->grtn', query_heads, all_keys) * score_scale
    positions = jnp.arange(comp_len, dtype=jnp.int32)
    own_allowed = positions[None, :] <= positions[:, None]
    allowed = jnp.concatenate([jnp.ones((comp_len, PROMPT), dtype=bool), own_allowed], 1)
    scores = jnp.where(allowed, scores, -jnp.inf)
    log_total = jax.nn.logsumexp(scores, axis=-1)
    prob_full = jnp.exp(scores - log_total[..., None])
    prob_half = lax.optimization_barrier(prob_full.astype(jnp.bfloat16)).astype(jnp.float32)
    output = jnp.einsum('grtn,ngd->grtd', prob_half, all_values)
    output = lax.optimization_barrier(output.astype(jnp.bfloat16)).astype(jnp.float32)
    row_delta = lax.optimization_barrier(jnp.sum(grad_heads * output, axis=-1))
    grad_prob = jnp.einsum('grtd,ngd->grtn', grad_heads, all_values)
    grad_score = score_scale * prob_full * (grad_prob - row_delta[..., None])
    grad_score = lax.optimization_barrier(grad_score.astype(jnp.bfloat16)).astype(jnp.float32)
    query_grad = jnp.einsum('grtn,ngd->grtd', grad_score, all_keys).transpose(2, 0, 1, 3).reshape(comp_len, -1)
    key_grad = jnp.einsum('grtn,grtd->ngd', grad_score, query_heads).reshape(-1, kv_width)
    value_grad = jnp.einsum('grtn,grtd->ngd', prob_half, grad_heads).reshape(-1, kv_width)
    return (query_grad, key_grad[PROMPT:], value_grad[PROMPT:], key_grad[:PROMPT], value_grad[:PROMPT])

def reference(queries, comp_keys, comp_values, prompt_keys, prompt_values, out_grad, lengths, loss_mask, buckets):
    weights = token_weights(lengths, loss_mask, buckets)
    cotangent = (weights[..., None] * out_grad.astype(jnp.float32)).astype(jnp.bfloat16)
    kv_width = KV_HEADS * HEAD_DIM

    def comp_step(carried, comp_items):
        query_rows, own_key, own_value, grad_rows = comp_items
        results = attend_one(query_rows, own_key, own_value, grad_rows, prompt_keys, prompt_values)
        return ((carried[0] + results[3], carried[1] + results[4]), (results[0], results[1], results[2]))
    start_sums = (jnp.zeros((PROMPT, kv_width), jnp.float32), jnp.zeros((PROMPT, kv_width), jnp.float32))
    prompt_sums, per_comp = lax.scan(comp_step, start_sums, (queries, comp_keys, comp_values, cotangent))
    return (per_comp[0], per_comp[1], per_comp[2], prompt_sums[0], prompt_sums[1])
```

```python
import functools

import jax
import jax.numpy as jnp
from jax import lax
from jax.experimental import pallas as pl
from jax.experimental.pallas import tpu as pltpu
from jax.sharding import PartitionSpec as P

HEAD_DIM = 128
SCALE = HEAD_DIM ** (-0.5)
LOG2E = 1.4426950408889634
META = 16
TILE = 256
NT = (((1,), (1,)), ((), ()))


def fold_rows(values, op):
    rows, cols = values.shape
    return op(values.reshape(rows // 8, 8, cols), axis=0)


def attention_kernel(
    members, row_chunk,
    gath, own_key, own_value, queries, grads, mine, mask,
    query_grad, own_key_grad, own_value_grad, prompt_grads,
    keys, values, keys_t, q_rows, g_rows, weight_row, scores, grad_prob, grad_score, key_acc, value_acc, dq_t,
):
    own_len = own_key.shape[0]
    comp_len, width = queries.shape
    heads = width // HEAD_DIM
    block = gath.shape[1] - META
    half = block // 2
    prompt_len = members * half
    total = prompt_len + own_len
    for i in range(members):
        keys[i * half:(i + 1) * half, :] = gath[i, :half, :]
        values[i * half:(i + 1) * half, :] = gath[i, half:block, :]
    keys[prompt_len:, :] = own_key[...]
    values[prompt_len:, :] = own_value[...]
    for i in range(total // 128):
        keys_t[:, i * 128:(i + 1) * 128] = keys[i * 128:(i + 1) * 128, :].T
    for h in range(heads):
        q_rows[h * comp_len:(h + 1) * comp_len, :] = queries[:, h * HEAD_DIM:(h + 1) * HEAD_DIM]
        g_rows[h * comp_len:(h + 1) * comp_len, :] = grads[:, h * HEAD_DIM:(h + 1) * HEAD_DIM]

    length_sum = jnp.zeros((1, 128), jnp.float32)
    reward_sum = jnp.zeros((1, 128), jnp.float32)
    square_sum = jnp.zeros((1, 128), jnp.float32)
    for i in range(members):
        meta = gath[i, block:block + META, :].astype(jnp.float32)
        reward = meta[1:2, :]
        length_sum += meta[0:1, :]
        reward_sum += reward
        square_sum += reward * reward
    own_meta = mine[block:block + META, :].astype(jnp.float32)
    reward_mean = reward_sum / members
    variance = square_sum / members - reward_mean * reward_mean
    advantage = (own_meta[1:2, :] - reward_mean) / jnp.sqrt(variance + 1.0)
    positions = lax.broadcasted_iota(jnp.int32, (1, comp_len), 1).astype(jnp.float32)
    valid = jnp.where(positions < own_meta[0:1, :], mask[...].astype(jnp.float32), 0.0)
    weights = advantage * valid * (members * comp_len / length_sum)
    weight_row[...] = jnp.concatenate([weights] * (TILE // comp_len), axis=1)

    chunks = total // row_chunk

    def tile_step(j, _):
        cols = pl.ds(pl.multiple_of(j * TILE, TILE), TILE)
        q_tile = q_rows[cols, :]
        g_tile = g_rows[cols, :]
        largest = jnp.full((8, TILE), -jnp.inf, jnp.float32)
        for i in range(chunks):
            rows = slice(i * row_chunk, (i + 1) * row_chunk)
            s = lax.dot_general(keys[rows, :], q_tile, NT, preferred_element_type=jnp.float32)
            if (i + 1) * row_chunk > prompt_len:
                own = s[row_chunk - own_len:, :]
                key_pos = lax.broadcasted_iota(jnp.int32, own.shape, 0)
                row_pos = lax.broadcasted_iota(jnp.int32, own.shape, 1) % comp_len
                own = jnp.where(key_pos <= row_pos, own, -jnp.inf)
                s = jnp.concatenate([s[:row_chunk - own_len, :], own], axis=0)
            scores[rows, :] = s
            largest = jnp.maximum(largest, fold_rows(s, jnp.max))
        top = jnp.max(largest, axis=0, keepdims=True)
        sums = jnp.zeros((8, TILE), jnp.float32)
        dots = jnp.zeros((8, TILE), jnp.float32)
        for i in range(chunks):
            rows = slice(i * row_chunk, (i + 1) * row_chunk)
            dp = lax.dot_general(values[rows, :], g_tile, NT, preferred_element_type=jnp.float32)
            e = jnp.exp2((scores[rows, :] - top) * (SCALE * LOG2E))
            scores[rows, :] = e
            grad_prob[rows, :] = dp
            sums += fold_rows(e, jnp.sum)
            dots += fold_rows(e * dp, jnp.sum)
        inverse = 1.0 / jnp.sum(sums, axis=0, keepdims=True)
        delta = jnp.sum(dots, axis=0, keepdims=True) * inverse
        factor = weight_row[...] * inverse
        for i in range(chunks):
            rows = slice(i * row_chunk, (i + 1) * row_chunk)
            p = scores[rows, :] * factor
            ds = (p * ((grad_prob[rows, :] - delta) * SCALE)).astype(jnp.bfloat16)
            grad_score[rows, :] = ds
            dv = jnp.dot(p.astype(jnp.bfloat16), g_tile, preferred_element_type=jnp.float32)
            dk = jnp.dot(ds, q_tile, preferred_element_type=jnp.float32)
            value_acc[rows, :] = jnp.where(j == 0, dv, value_acc[rows, :] + dv)
            key_acc[rows, :] = jnp.where(j == 0, dk, key_acc[rows, :] + dk)
        dq_t[j] = jnp.dot(keys_t[...], grad_score[...], preferred_element_type=jnp.float32)
        return 0

    key_acc[...] = jnp.zeros_like(key_acc)
    value_acc[...] = jnp.zeros_like(value_acc)
    lax.fori_loop(0, width // TILE, tile_step, 0)

    for h in range(heads):
        j, k = divmod(h * HEAD_DIM, TILE)
        query_grad[:, h * HEAD_DIM:(h + 1) * HEAD_DIM] = dq_t[j, :, k:k + HEAD_DIM].T
    for i in range(members):
        prompt_grads[i, :half, :] = key_acc[i * half:(i + 1) * half, :].astype(jnp.bfloat16)
        prompt_grads[i, half:, :] = value_acc[i * half:(i + 1) * half, :].astype(jnp.bfloat16)
    own_key_grad[...] = key_acc[prompt_len:, :]
    own_value_grad[...] = value_acc[prompt_len:, :]


def attention(gath, own_key, own_value, queries, grads, mine, mask):
    members, packed, dim = gath.shape
    block = packed - META
    comp_len, width = queries.shape
    own_len = own_key.shape[0]
    total = members * block // 2 + own_len
    f32, bf16 = jnp.float32, jnp.bfloat16
    vmem = pl.BlockSpec(memory_space=pltpu.VMEM)
    row_chunk = 544
    units = total * comp_len * width
    return pl.pallas_call(
        functools.partial(attention_kernel, members, row_chunk),
        out_shape=(
            jax.ShapeDtypeStruct((comp_len, width), f32),
            jax.ShapeDtypeStruct((own_len, dim), f32),
            jax.ShapeDtypeStruct((own_len, dim), f32),
            jax.ShapeDtypeStruct((members, block, dim), bf16),
        ),
        in_specs=[vmem] * 7,
        out_specs=(vmem,) * 4,
        scratch_shapes=[
            pltpu.VMEM((total, dim), bf16),
            pltpu.VMEM((total, dim), bf16),
            pltpu.VMEM((dim, total), bf16),
            pltpu.VMEM((width, dim), bf16),
            pltpu.VMEM((width, dim), bf16),
            pltpu.VMEM((1, TILE), f32),
            pltpu.VMEM((total, TILE), f32),
            pltpu.VMEM((total, TILE), f32),
            pltpu.VMEM((total, TILE), bf16),
            pltpu.VMEM((total, dim), f32),
            pltpu.VMEM((total, dim), f32),
            pltpu.VMEM((width // TILE, dim, TILE), f32),
        ],
        compiler_params=pltpu.CompilerParams(vmem_limit_bytes=32 * 1024 * 1024),
        cost_estimate=pl.CostEstimate(flops=10 * units, bytes_accessed=4 * units // 100, transcendentals=total * width),
        name="attention",
    )(gath, own_key, own_value, queries, grads, mine, mask)


def body(queries, comp_keys, comp_values, prompt_keys, prompt_values, out_grad, lengths, loss_mask, buckets):
    along_x = lax.axis_size("gx")
    dim = prompt_keys.shape[1]
    row = lax.broadcasted_iota(jnp.int32, (META, dim), 0)
    meta = jnp.where(row == 0, lengths[0], jnp.where(row == 1, buckets[0], 0)).astype(jnp.bfloat16)
    mine = jnp.concatenate([prompt_keys, prompt_values, meta], axis=0)
    column = lax.all_gather(mine, "gz")
    gath = lax.all_to_all(jnp.broadcast_to(column[None], (along_x, *column.shape)), "gx", 0, 0)
    gath = gath.reshape(-1, *mine.shape)
    query_grad, own_key_grad, own_value_grad, prompt_grads = attention(
        gath, comp_keys[0], comp_values[0], queries[0], out_grad[0], mine, loss_mask
    )
    prompt_grads = prompt_grads.reshape(along_x, -1, *prompt_grads.shape[1:])
    terms = lax.all_to_all(prompt_grads, "gx", 0, 0)
    partial = jnp.sum(terms.astype(jnp.float32), axis=0).astype(jnp.bfloat16)
    terms = lax.all_to_all(partial, "gz", 0, 0)
    owned = jnp.sum(terms.astype(jnp.float32), axis=0)
    half = owned.shape[0] // 2
    return (
        query_grad[None],
        own_key_grad[None],
        own_value_grad[None],
        owned[:half],
        owned[half:],
    )


def solution(mesh):
    dp, group, tensor = (mesh.shape[name] for name in ("dp", "group", "tensor"))
    along_z = 4
    split = jax.sharding.Mesh(
        mesh.devices.reshape(dp, group // along_z, along_z, tensor), ("dp", "gx", "gz", "tensor")
    )
    rows = ("dp", "gx", "gz")
    return jax.shard_map(
        body,
        mesh=split,
        in_specs=(
            P(rows, None, "tensor"),
            P(rows, None, "tensor"),
            P(rows, None, "tensor"),
            P(rows, "tensor"),
            P(rows, "tensor"),
            P(rows, None, "tensor"),
            P(rows),
            P(rows, None),
            P(rows),
        ),
        out_specs=(
            P(rows, None, "tensor"),
            P(rows, None, "tensor"),
            P(rows, None, "tensor"),
            P(rows, "tensor"),
            P(rows, "tensor"),
        ),
        check_vma=False,
    )
```

```python
import functools

import jax
import jax.numpy as jnp
from jax import lax
from jax.experimental import pallas as pl
from jax.experimental.pallas import tpu as pltpu
from jax.sharding import PartitionSpec as P

HEAD_DIM = 128
SCALE = HEAD_DIM ** (-0.5)
LOG2E = 1.4426950408889634
META = 16
Z_ORDER = [2, 1, 0, 3]
TILE = 512
NT = (((1,), (1,)), ((), ()))


def fold_rows(values, op):
    rows, cols = values.shape
    return op(values.reshape(rows // 8, 8, cols), axis=0)


def attention_kernel(
    members, row_chunk,
    gath, own_key, own_value, queries, grads, mine, mask,
    query_grad, own_key_grad, own_value_grad, prompt_grads,
    keys, values, keys_t, q_rows, g_rows, weight_row, scores, grad_prob, expo, grad_score, key_acc, value_acc, dq_t,
):
    own_len = own_key.shape[0]
    comp_len, width = queries.shape
    heads = width // HEAD_DIM
    block = gath.shape[1] - META
    half = block // 2
    prompt_len = members * half
    total = prompt_len + own_len
    for i in range(members):
        keys[i * half:(i + 1) * half, :] = gath[i, :half, :]
        values[i * half:(i + 1) * half, :] = gath[i, half:block, :]
    keys[prompt_len:, :] = own_key[...]
    values[prompt_len:, :] = own_value[...]
    for i in range(total // 128):
        keys_t[:, i * 128:(i + 1) * 128] = keys[i * 128:(i + 1) * 128, :].T
    for h in range(heads):
        q_rows[h * comp_len:(h + 1) * comp_len, :] = queries[:, h * HEAD_DIM:(h + 1) * HEAD_DIM]
        g_rows[h * comp_len:(h + 1) * comp_len, :] = grads[:, h * HEAD_DIM:(h + 1) * HEAD_DIM]

    length_sum = jnp.zeros((1, 128), jnp.float32)
    reward_sum = jnp.zeros((1, 128), jnp.float32)
    square_sum = jnp.zeros((1, 128), jnp.float32)
    for i in range(members):
        meta = gath[i, block:block + META, :].astype(jnp.float32)
        reward = meta[1:2, :]
        length_sum += meta[0:1, :]
        reward_sum += reward
        square_sum += reward * reward
    own_meta = mine[block:block + META, :].astype(jnp.float32)
    reward_mean = reward_sum / members
    variance = square_sum / members - reward_mean * reward_mean
    advantage = (own_meta[1:2, :] - reward_mean) / jnp.sqrt(variance + 1.0)
    positions = lax.broadcasted_iota(jnp.int32, (1, comp_len), 1).astype(jnp.float32)
    valid = jnp.where(positions < own_meta[0:1, :], mask[...].astype(jnp.float32), 0.0)
    weights = advantage * valid * (members * comp_len / length_sum)
    weight_row[...] = jnp.concatenate([weights] * (TILE // comp_len), axis=1)

    chunks = total // row_chunk

    def tile_step(j):
        cols = slice(j * TILE, (j + 1) * TILE)
        q_tile = q_rows[cols, :]
        g_tile = g_rows[cols, :]
        largest = jnp.full((8, TILE), -jnp.inf, jnp.float32)
        for i in range(chunks):
            rows = slice(i * row_chunk, (i + 1) * row_chunk)
            s = lax.dot_general(keys[rows, :], q_tile, NT, preferred_element_type=jnp.float32)
            if (i + 1) * row_chunk > prompt_len:
                own = s[row_chunk - own_len:, :]
                key_pos = lax.broadcasted_iota(jnp.int32, own.shape, 0)
                row_pos = lax.broadcasted_iota(jnp.int32, own.shape, 1) % comp_len
                own = jnp.where(key_pos <= row_pos, own, -jnp.inf)
                s = jnp.concatenate([s[:row_chunk - own_len, :], own], axis=0)
            scores[rows, :] = s
            largest = jnp.maximum(largest, fold_rows(s, jnp.max))
        top = jnp.max(largest, axis=0, keepdims=True)
        sums = jnp.zeros((8, TILE), jnp.float32)
        dots = jnp.zeros((8, TILE), jnp.float32)
        for i in range(chunks):
            rows = slice(i * row_chunk, (i + 1) * row_chunk)
            dp = lax.dot_general(values[rows, :], g_tile, NT, preferred_element_type=jnp.float32)
            e = jnp.exp2((scores[rows, :] - top) * (SCALE * LOG2E))
            expo[rows, :] = e.astype(jnp.bfloat16)
            grad_prob[rows, :] = dp
            sums += fold_rows(e, jnp.sum)
            dots += fold_rows(e * dp, jnp.sum)
        inverse = 1.0 / jnp.sum(sums, axis=0, keepdims=True)
        delta = jnp.sum(dots, axis=0, keepdims=True) * inverse
        factor = weight_row[...] * inverse
        column = jnp.concatenate(
            [jnp.broadcast_to(factor[:, k:k + 128], (128, 128)).T for k in range(0, TILE, 128)], axis=0
        )
        g_scaled = (g_tile.astype(jnp.float32) * column).astype(jnp.bfloat16)
        q_scaled = (q_tile.astype(jnp.float32) * (column * SCALE)).astype(jnp.bfloat16)
        for i in range(chunks):
            rows = slice(i * row_chunk, (i + 1) * row_chunk)
            e = expo[rows, :]
            ds = (e.astype(jnp.float32) * (grad_prob[rows, :] - delta)).astype(jnp.bfloat16)
            grad_score[rows, :] = ds
            dv = jnp.dot(e, g_scaled, preferred_element_type=jnp.float32)
            dk = jnp.dot(ds, q_scaled, preferred_element_type=jnp.float32)
            value_acc[rows, :] = dv if j == 0 else value_acc[rows, :] + dv
            key_acc[rows, :] = dk if j == 0 else key_acc[rows, :] + dk
        dq = jnp.dot(keys_t[...], grad_score[...], preferred_element_type=jnp.float32)
        dq_t[j] = dq * (factor * SCALE)

    for j in range(width // TILE):
        tile_step(j)

    for h in range(heads):
        j, k = divmod(h * HEAD_DIM, TILE)
        query_grad[:, h * HEAD_DIM:(h + 1) * HEAD_DIM] = dq_t[j, :, k:k + HEAD_DIM].T
    for i in range(members):
        prompt_grads[i, :half, :] = key_acc[i * half:(i + 1) * half, :].astype(jnp.bfloat16)
        prompt_grads[i, half:, :] = value_acc[i * half:(i + 1) * half, :].astype(jnp.bfloat16)
    own_key_grad[...] = key_acc[prompt_len:, :]
    own_value_grad[...] = value_acc[prompt_len:, :]


def attention(gath, own_key, own_value, queries, grads, mine, mask):
    members, packed, dim = gath.shape
    block = packed - META
    comp_len, width = queries.shape
    own_len = own_key.shape[0]
    total = members * block // 2 + own_len
    f32, bf16 = jnp.float32, jnp.bfloat16
    vmem = pl.BlockSpec(memory_space=pltpu.VMEM)
    row_chunk = 544
    units = total * comp_len * width
    return pl.pallas_call(
        functools.partial(attention_kernel, members, row_chunk),
        out_shape=(
            jax.ShapeDtypeStruct((comp_len, width), f32),
            jax.ShapeDtypeStruct((own_len, dim), f32),
            jax.ShapeDtypeStruct((own_len, dim), f32),
            jax.ShapeDtypeStruct((members, block, dim), bf16),
        ),
        in_specs=[vmem] * 7,
        out_specs=(vmem,) * 4,
        scratch_shapes=[
            pltpu.VMEM((total, dim), bf16),
            pltpu.VMEM((total, dim), bf16),
            pltpu.VMEM((dim, total), bf16),
            pltpu.VMEM((width, dim), bf16),
            pltpu.VMEM((width, dim), bf16),
            pltpu.VMEM((1, TILE), f32),
            pltpu.VMEM((total, TILE), f32),
            pltpu.VMEM((total, TILE), f32),
            pltpu.VMEM((total, TILE), bf16),
            pltpu.VMEM((total, TILE), bf16),
            pltpu.VMEM((total, dim), f32),
            pltpu.VMEM((total, dim), f32),
            pltpu.VMEM((width // TILE, dim, TILE), f32),
        ],
        compiler_params=pltpu.CompilerParams(vmem_limit_bytes=32 * 1024 * 1024),
        cost_estimate=pl.CostEstimate(flops=10 * units, bytes_accessed=4 * units // 100, transcendentals=total * width),
        name="attention",
    )(gath, own_key, own_value, queries, grads, mine, mask)


def body(queries, comp_keys, comp_values, prompt_keys, prompt_values, out_grad, lengths, loss_mask, buckets):
    along_x = lax.axis_size("gx")
    row = lax.broadcasted_iota(jnp.int32, (META, prompt_keys.shape[1]), 0)
    meta = jnp.where(row == 0, lengths[0], jnp.where(row == 1, buckets[0], 0)).astype(jnp.bfloat16)
    mine = jnp.concatenate([prompt_keys, prompt_values, meta], axis=0)
    column = lax.all_gather(mine, "gz")
    gath = lax.all_to_all(jnp.broadcast_to(column[None], (along_x, *column.shape)), "gx", 0, 0)
    gath = gath.reshape(-1, *mine.shape)
    query_grad, own_key_grad, own_value_grad, prompt_grads = attention(
        gath, comp_keys[0], comp_values[0], queries[0], out_grad[0], mine, loss_mask
    )
    prompt_grads = prompt_grads.reshape(along_x, -1, *prompt_grads.shape[1:])
    terms = lax.all_to_all(prompt_grads, "gx", 0, 0)
    partial = jnp.sum(terms.astype(jnp.float32), axis=0).astype(jnp.bfloat16)
    terms = lax.all_to_all(jnp.stack([partial[i] for i in Z_ORDER]), "gz", 0, 0, axis_index_groups=[Z_ORDER])
    owned = jnp.sum(terms.astype(jnp.float32), axis=0)
    half = owned.shape[0] // 2
    return (
        query_grad[None],
        own_key_grad[None],
        own_value_grad[None],
        owned[:half],
        owned[half:],
    )


def solution(mesh):
    dp, group, tensor = (mesh.shape[name] for name in ("dp", "group", "tensor"))
    along_z = 4
    split = jax.sharding.Mesh(
        mesh.devices.reshape(dp, group // along_z, along_z, tensor), ("dp", "gx", "gz", "tensor")
    )
    rows = ("dp", "gx", "gz")
    return jax.shard_map(
        body,
        mesh=split,
        in_specs=(
            P(rows, None, "tensor"),
            P(rows, None, "tensor"),
            P(rows, None, "tensor"),
            P(rows, "tensor"),
            P(rows, "tensor"),
            P(rows, None, "tensor"),
            P(rows),
            P(rows, None),
            P(rows),
        ),
        out_specs=(
            P(rows, None, "tensor"),
            P(rows, None, "tensor"),
            P(rows, None, "tensor"),
            P(rows, "tensor"),
            P(rows, "tensor"),
        ),
        check_vma=False,
    )
```

```python
import jax
import jax.numpy as jnp
from jax import lax
from jax.experimental import pallas as pl
from jax.experimental.pallas import tpu as pltpu
from jax.sharding import PartitionSpec as P

HEAD_DIM = 128
SCALE = HEAD_DIM ** (-0.5)
LOG2E = 1.4426950408889634
META = 16
Z_ORDER = [2, 1, 0, 3]
SHIFTS = (0, 1, 3, 2)
TILE = 512
NT = (((1,), (1,)), ((), ()))


def fold_rows(values, op):
    rows, cols = values.shape
    return op(values.reshape(rows // 8, 8, cols), axis=0)


def copy_column(column, key_rows, value_rows, start):
    blocks, packed, _ = column.shape
    half = (packed - META) // 2
    for i in range(blocks):
        rows = slice(start + i * half, start + (i + 1) * half)
        key_rows[rows, :] = column[i, :half, :]
        value_rows[rows, :] = column[i, half:2 * half, :]


def transpose_rows(rows_ref, out):
    for i in range(0, rows_ref.shape[0], 128):
        out[:, i:i + 128] = rows_ref[i:i + 128, :].T


def forward_tile(cols, key_rows, value_rows, q_tile, g_tile, scores, expo, grad_prob, stats, own_len, comp_len):
    total = key_rows.shape[0]
    width = q_tile.shape[0]
    chunk = 512 if total % 512 == 0 else total // 2
    largest = jnp.full((8, width), -jnp.inf, jnp.float32)
    for i in range(0, total, chunk):
        rows = slice(i, i + chunk)
        s = lax.dot_general(key_rows[rows, :], q_tile, NT, preferred_element_type=jnp.float32)
        if own_len and i + chunk == total:
            own = s[chunk - own_len:, :]
            key_pos = lax.broadcasted_iota(jnp.int32, own.shape, 0)
            row_pos = lax.broadcasted_iota(jnp.int32, own.shape, 1) % comp_len
            own = jnp.where(key_pos <= row_pos, own, -jnp.inf)
            s = jnp.concatenate([s[:chunk - own_len, :], own], axis=0)
        scores[rows, :] = s
        largest = jnp.maximum(largest, fold_rows(s, jnp.max))
    top = jnp.max(largest, axis=0, keepdims=True)
    sums = jnp.zeros((8, width), jnp.float32)
    dots = jnp.zeros((8, width), jnp.float32)
    for i in range(0, total, chunk):
        rows = slice(i, i + chunk)
        dp = lax.dot_general(value_rows[rows, :], g_tile, NT, preferred_element_type=jnp.float32)
        e = jnp.exp2((scores[rows, :] - top) * (SCALE * LOG2E))
        expo[rows, cols] = e.astype(jnp.bfloat16)
        grad_prob[rows, cols] = dp
        sums += fold_rows(e, jnp.sum)
        dots += fold_rows(e * dp, jnp.sum)
    stats[0:8, cols] = jnp.broadcast_to(top, (8, width))
    stats[8:16, cols] = sums
    stats[16:24, cols] = dots


def tiles_of(width):
    return [slice(j, j + TILE) for j in range(0, width, TILE)]


def own_kernel(
    column, own_key, own_value, queries, grads,
    q_rows, g_rows, keys_t, expo, grad_prob, stats,
    key_rows, value_rows, scores,
):
    comp_len, width = queries.shape
    own_len = own_key.shape[0]
    for h in range(width // HEAD_DIM):
        q_rows[h * comp_len:(h + 1) * comp_len, :] = queries[:, h * HEAD_DIM:(h + 1) * HEAD_DIM]
        g_rows[h * comp_len:(h + 1) * comp_len, :] = grads[:, h * HEAD_DIM:(h + 1) * HEAD_DIM]
    copy_column(column, key_rows, value_rows, 0)
    start = key_rows.shape[0] - own_len
    key_rows[start:, :] = own_key[...]
    value_rows[start:, :] = own_value[...]
    transpose_rows(key_rows, keys_t)
    for cols in tiles_of(width):
        forward_tile(
            cols, key_rows, value_rows, q_rows[cols, :], g_rows[cols, :],
            scores, expo, grad_prob, stats, own_len, comp_len,
        )


def near_kernel(
    column, q_rows, g_rows,
    keys_t, expo, grad_prob, stats,
    key_rows, value_rows, scores,
):
    copy_column(column, key_rows, value_rows, 0)
    transpose_rows(key_rows, keys_t)
    for cols in tiles_of(q_rows.shape[0]):
        forward_tile(
            cols, key_rows, value_rows, q_rows[cols, :], g_rows[cols, :],
            scores, expo, grad_prob, stats, 0, 0,
        )


def last_kernel(
    place, columns_0, columns_1, columns_2, columns_3, mine, mask, q_rows, g_rows,
    keys_t0, expo_0, grad_prob_0, stats_0, keys_t1, expo_1, grad_prob_1, stats_1,
    keys_t2, expo_2, grad_prob_2, stats_2,
    query_grad, own_key_grad, own_value_grad, prompt_grads,
    key_rows, value_rows, keys_t3, expo_3, grad_prob_3, stats_3, scores, grad_score, key_acc, value_acc, dq_t,
):
    columns = (columns_0, columns_1, columns_2, columns_3)
    along_x, along_z = len(columns), columns_0.shape[0]
    block = columns_0.shape[1] - META
    half = block // 2
    width = q_rows.shape[0]
    comp_len = mask.shape[1]
    members = along_x * along_z

    length_sum = jnp.zeros((1, 128), jnp.float32)
    reward_sum = jnp.zeros((1, 128), jnp.float32)
    square_sum = jnp.zeros((1, 128), jnp.float32)
    for column in columns:
        for i in range(along_z):
            meta = column[i, block:block + META, :].astype(jnp.float32)
            reward = meta[1:2, :]
            length_sum += meta[0:1, :]
            reward_sum += reward
            square_sum += reward * reward
    own_meta = mine[block:block + META, :].astype(jnp.float32)
    reward_mean = reward_sum / members
    variance = square_sum / members - reward_mean * reward_mean
    advantage = (own_meta[1:2, :] - reward_mean) / jnp.sqrt(variance + 1.0)
    positions = lax.broadcasted_iota(jnp.int32, (1, comp_len), 1).astype(jnp.float32)
    valid = jnp.where(positions < own_meta[0:1, :], mask[...].astype(jnp.float32), 0.0)
    weights = advantage * valid * (members * comp_len / length_sum)
    weight_row = jnp.concatenate([weights] * (TILE // comp_len), axis=1)

    copy_column(columns[3], key_rows, value_rows, 0)
    transpose_rows(key_rows, keys_t3)
    groups = (
        (keys_t0, expo_0, grad_prob_0, stats_0),
        (keys_t1, expo_1, grad_prob_1, stats_1),
        (keys_t2, expo_2, grad_prob_2, stats_2),
        (keys_t3, expo_3, grad_prob_3, stats_3),
    )
    for j, cols in enumerate(tiles_of(width)):
        q_tile = q_rows[cols, :]
        g_tile = g_rows[cols, :]
        forward_tile(cols, key_rows, value_rows, q_tile, g_tile, scores, expo_3, grad_prob_3, stats_3, 0, 0)
        tops = [stats[0:1, cols] for *_, stats in groups]
        top = jnp.maximum(jnp.maximum(tops[0], tops[1]), jnp.maximum(tops[2], tops[3]))
        shares = [jnp.exp2((t - top) * (SCALE * LOG2E)) for t in tops]
        sums = sum(share * stats[8:16, cols] for share, (*_, stats) in zip(shares, groups))
        dots = sum(share * stats[16:24, cols] for share, (*_, stats) in zip(shares, groups))
        inverse = 1.0 / jnp.sum(sums, axis=0, keepdims=True)
        delta = jnp.sum(dots, axis=0, keepdims=True) * inverse
        factor = weight_row * inverse
        dq = None
        start = 0
        for share, (keys_t, expo, grad_prob, _) in zip(shares, groups):
            part = factor * share
            column = jnp.concatenate(
                [jnp.broadcast_to(part[:, k:k + 128], (128, 128)).T for k in range(0, TILE, 128)], axis=0
            )
            g_scaled = (g_tile.astype(jnp.float32) * column).astype(jnp.bfloat16)
            q_scaled = (q_tile.astype(jnp.float32) * (column * SCALE)).astype(jnp.bfloat16)
            total = keys_t.shape[1]
            chunk = 512 if total % 512 == 0 else total // 2
            for i in range(0, total, chunk):
                rows = slice(i, i + chunk)
                out = slice(start + i, start + i + chunk)
                e = expo[rows, cols]
                ds = (e.astype(jnp.float32) * (grad_prob[rows, cols] - delta)).astype(jnp.bfloat16)
                grad_score[out, :] = ds
                dv = jnp.dot(e, g_scaled, preferred_element_type=jnp.float32)
                dk = jnp.dot(ds, q_scaled, preferred_element_type=jnp.float32)
                value_acc[out, :] = dv if j == 0 else value_acc[out, :] + dv
                key_acc[out, :] = dk if j == 0 else key_acc[out, :] + dk
            some = jnp.dot(keys_t[...], grad_score[start:start + total, :], preferred_element_type=jnp.float32)
            some = some * (part * SCALE)
            dq = some if dq is None else dq + some
            start += total
        dq_t[j] = dq

    for h in range(width // HEAD_DIM):
        j, k = divmod(h * HEAD_DIM, TILE)
        query_grad[:, h * HEAD_DIM:(h + 1) * HEAD_DIM] = dq_t[j, :, k:k + HEAD_DIM].T
    own_start = along_z * half
    own_len = own_key_grad.shape[0]
    own_key_grad[...] = key_acc[own_start:own_start + own_len, :]
    own_value_grad[...] = value_acc[own_start:own_start + own_len, :]
    starts = [0] + [own_start + own_len + k * own_start for k in range(along_x - 1)]
    for start, shift in zip(starts, SHIFTS):
        target = lax.rem(place[0] + (along_x - shift), along_x)
        for i in range(along_z):
            rows = slice(start + i * half, start + (i + 1) * half)
            prompt_grads[target, i, :half, :] = key_acc[rows, :].astype(jnp.bfloat16)
            prompt_grads[target, i, half:, :] = value_acc[rows, :].astype(jnp.bfloat16)


def forward_outputs(total, width):
    return (
        jax.ShapeDtypeStruct((HEAD_DIM, total), jnp.bfloat16),
        jax.ShapeDtypeStruct((total, width), jnp.bfloat16),
        jax.ShapeDtypeStruct((total, width), jnp.float32),
        jax.ShapeDtypeStruct((24, width), jnp.float32),
    )


def scratch(total):
    return [
        pltpu.VMEM((total, HEAD_DIM), jnp.bfloat16),
        pltpu.VMEM((total, HEAD_DIM), jnp.bfloat16),
    ]


VMEM = pl.BlockSpec(memory_space=pltpu.VMEM)


def params(mebibytes):
    return pltpu.CompilerParams(vmem_limit_bytes=mebibytes * 1024 * 1024)


def cost(total, width, passes):
    units = total * width
    return pl.CostEstimate(flops=2 * HEAD_DIM * units * passes, bytes_accessed=0, transcendentals=units)


def own_forward(column, own_key, own_value, queries, grads):
    width = queries.shape[1]
    total = column.shape[0] * (column.shape[1] - META) // 2 + own_key.shape[0]
    rows = jax.ShapeDtypeStruct((width, HEAD_DIM), jnp.bfloat16)
    outs = (rows, rows, *forward_outputs(total, width))
    return pl.pallas_call(
        own_kernel,
        out_shape=outs,
        in_specs=[VMEM] * 5,
        out_specs=(VMEM,) * len(outs),
        scratch_shapes=[*scratch(total), pltpu.VMEM((total, TILE), jnp.float32)],
        compiler_params=params(24),
        cost_estimate=cost(total, width, 2),
        name="own_forward",
    )(column, own_key, own_value, queries, grads)


def near_forward(column, q_rows, g_rows):
    width = q_rows.shape[0]
    total = column.shape[0] * (column.shape[1] - META) // 2
    outs = forward_outputs(total, width)
    return pl.pallas_call(
        near_kernel,
        out_shape=outs,
        in_specs=[VMEM] * 3,
        out_specs=(VMEM,) * len(outs),
        scratch_shapes=[*scratch(total), pltpu.VMEM((total, TILE), jnp.float32)],
        compiler_params=params(24),
        cost_estimate=cost(total, width, 2),
        name="near_forward",
    )(column, q_rows, g_rows)


def last_and_backward(place, columns, mine, mask, q_rows, g_rows, own_state, near_state):
    width = q_rows.shape[0]
    along_z, packed, dim = columns[0].shape
    block = packed - META
    comp_len = mask.shape[1]
    column_rows = along_z * block // 2
    own_len = own_state[0].shape[1] - column_rows
    total = len(columns) * column_rows + own_len
    f32, bf16 = jnp.float32, jnp.bfloat16
    state = [*own_state, *near_state]
    return pl.pallas_call(
        last_kernel,
        out_shape=(
            jax.ShapeDtypeStruct((comp_len, width), f32),
            jax.ShapeDtypeStruct((own_len, dim), f32),
            jax.ShapeDtypeStruct((own_len, dim), f32),
            jax.ShapeDtypeStruct((len(columns), along_z, block, dim), bf16),
        ),
        in_specs=[pl.BlockSpec(memory_space=pltpu.SMEM)] + [VMEM] * (len(columns) + 4 + len(state)),
        out_specs=(VMEM,) * 4,
        scratch_shapes=[
            *scratch(column_rows),
            *[pltpu.VMEM(out.shape, out.dtype) for out in forward_outputs(column_rows, width)],
            pltpu.VMEM((column_rows, TILE), f32),
            pltpu.VMEM((total, TILE), bf16),
            pltpu.VMEM((total, dim), f32),
            pltpu.VMEM((total, dim), f32),
            pltpu.VMEM((width // TILE, dim, TILE), f32),
        ],
        compiler_params=params(36),
        cost_estimate=cost(total, width, 4),
        name="last_and_backward",
    )(place, *columns, mine, mask, q_rows, g_rows, *state)


def shifted(column, shift):
    size = lax.axis_size("gx")
    return lax.ppermute(column, "gx", [(i, (i + shift) % size) for i in range(size)])


def body(queries, comp_keys, comp_values, prompt_keys, prompt_values, out_grad, lengths, loss_mask, buckets):
    row = lax.broadcasted_iota(jnp.int32, (META, prompt_keys.shape[1]), 0)
    meta = jnp.where(row == 0, lengths[0], jnp.where(row == 1, buckets[0], 0)).astype(jnp.bfloat16)
    mine = jnp.concatenate([prompt_keys, prompt_values, meta], axis=0)
    column = lax.all_gather(mine, "gz")
    columns = [column] + [None] * 3
    for k in (3, 1, 2):
        columns[k] = shifted(column, SHIFTS[k])
    q_rows, g_rows, *own_state = own_forward(column, comp_keys[0], comp_values[0], queries[0], out_grad[0])
    near_state = [*near_forward(columns[1], q_rows, g_rows), *near_forward(columns[2], q_rows, g_rows)]
    place = lax.axis_index("gx").astype(jnp.int32)[None]
    query_grad, own_key_grad, own_value_grad, prompt_grads = last_and_backward(
        place, columns, mine, loss_mask, q_rows, g_rows, own_state, near_state
    )
    terms = lax.all_to_all(prompt_grads, "gx", 0, 0)
    partial = jnp.sum(terms.astype(jnp.float32), axis=0).astype(jnp.bfloat16)
    terms = lax.all_to_all(jnp.stack([partial[i] for i in Z_ORDER]), "gz", 0, 0, axis_index_groups=[Z_ORDER])
    owned = jnp.sum(terms.astype(jnp.float32), axis=0)
    half = owned.shape[0] // 2
    return (
        query_grad[None],
        own_key_grad[None],
        own_value_grad[None],
        owned[:half],
        owned[half:],
    )


def solution(mesh):
    dp, group, tensor = (mesh.shape[name] for name in ("dp", "group", "tensor"))
    along_z = 4
    split = jax.sharding.Mesh(
        mesh.devices.reshape(dp, group // along_z, along_z, tensor), ("dp", "gx", "gz", "tensor")
    )
    rows = ("dp", "gx", "gz")
    return jax.shard_map(
        body,
        mesh=split,
        in_specs=(
            P(rows, None, "tensor"),
            P(rows, None, "tensor"),
            P(rows, None, "tensor"),
            P(rows, "tensor"),
            P(rows, "tensor"),
            P(rows, None, "tensor"),
            P(rows),
            P(rows, None),
            P(rows),
        ),
        out_specs=(
            P(rows, None, "tensor"),
            P(rows, None, "tensor"),
            P(rows, None, "tensor"),
            P(rows, "tensor"),
            P(rows, "tensor"),
        ),
        check_vma=False,
    )
```

```python
import jax
import jax.numpy as jnp
from jax import lax
from jax.experimental import pallas as pl
from jax.experimental.pallas import tpu as pltpu
from jax.sharding import PartitionSpec as P

HEAD_DIM = 128
SCALE = HEAD_DIM ** (-0.5)
LOG2E = 1.4426950408889634
META = 16
Z_ORDER = [2, 1, 0, 3]
SHIFTS = (0, 1, 3, 2)
TILE = 512
NT = (((1,), (1,)), ((), ()))


def fold_rows(values, op):
    rows, cols = values.shape
    return op(values.reshape(rows // 8, 8, cols), axis=0)


def copy_column(column, key_rows, value_rows, start):
    blocks, packed, _ = column.shape
    half = (packed - META) // 2
    for i in range(blocks):
        rows = slice(start + i * half, start + (i + 1) * half)
        key_rows[rows, :] = column[i, :half, :]
        value_rows[rows, :] = column[i, half:2 * half, :]


def transpose_rows(rows_ref, out):
    for i in range(0, rows_ref.shape[0], 128):
        out[:, i:i + 128] = rows_ref[i:i + 128, :].T


def forward_tile(cols, key_rows, value_rows, q_tile, g_tile, scores, expo, grad_prob, stats, own_len, comp_len):
    total = key_rows.shape[0]
    width = q_tile.shape[0]
    chunk = 512 if total % 512 == 0 else total // 2
    largest = jnp.full((8, width), -jnp.inf, jnp.float32)
    for i in range(0, total, chunk):
        rows = slice(i, i + chunk)
        s = lax.dot_general(key_rows[rows, :], q_tile, NT, preferred_element_type=jnp.float32)
        if own_len and i + chunk == total:
            own = s[chunk - own_len:, :]
            key_pos = lax.broadcasted_iota(jnp.int32, own.shape, 0)
            row_pos = lax.broadcasted_iota(jnp.int32, own.shape, 1) % comp_len
            own = jnp.where(key_pos <= row_pos, own, -jnp.inf)
            s = jnp.concatenate([s[:chunk - own_len, :], own], axis=0)
        scores[rows, :] = s
        largest = jnp.maximum(largest, fold_rows(s, jnp.max))
    top = jnp.max(largest, axis=0, keepdims=True)
    sums = jnp.zeros((8, width), jnp.float32)
    dots = jnp.zeros((8, width), jnp.float32)
    for i in range(0, total, chunk):
        rows = slice(i, i + chunk)
        dp = lax.dot_general(value_rows[rows, :], g_tile, NT, preferred_element_type=jnp.float32)
        e = jnp.exp2((scores[rows, :] - top) * (SCALE * LOG2E))
        expo[rows, cols] = e.astype(jnp.bfloat16)
        grad_prob[rows, cols] = dp
        sums += fold_rows(e, jnp.sum)
        dots += fold_rows(e * dp, jnp.sum)
    stats[0:8, cols] = jnp.broadcast_to(top, (8, width))
    stats[8:16, cols] = sums
    stats[16:24, cols] = dots


def tiles_of(width):
    return [slice(j, j + TILE) for j in range(0, width, TILE)]


def own_kernel(
    column, own_key, own_value, queries, grads,
    q_rows, g_rows, keys_t, expo, grad_prob, stats,
    key_rows, value_rows, scores,
):
    comp_len, width = queries.shape
    own_len = own_key.shape[0]
    for h in range(width // HEAD_DIM):
        q_rows[h * comp_len:(h + 1) * comp_len, :] = queries[:, h * HEAD_DIM:(h + 1) * HEAD_DIM]
        g_rows[h * comp_len:(h + 1) * comp_len, :] = grads[:, h * HEAD_DIM:(h + 1) * HEAD_DIM]
    copy_column(column, key_rows, value_rows, 0)
    start = key_rows.shape[0] - own_len
    key_rows[start:, :] = own_key[...]
    value_rows[start:, :] = own_value[...]
    transpose_rows(key_rows, keys_t)
    for cols in tiles_of(width):
        forward_tile(
            cols, key_rows, value_rows, q_rows[cols, :], g_rows[cols, :],
            scores, expo, grad_prob, stats, own_len, comp_len,
        )


def near_kernel(
    column, q_rows, g_rows,
    keys_t, expo, grad_prob, stats,
    key_rows, value_rows, scores,
):
    copy_column(column, key_rows, value_rows, 0)
    transpose_rows(key_rows, keys_t)
    for cols in tiles_of(q_rows.shape[0]):
        forward_tile(
            cols, key_rows, value_rows, q_rows[cols, :], g_rows[cols, :],
            scores, expo, grad_prob, stats, 0, 0,
        )


def last_kernel(
    place, columns_0, columns_1, columns_2, columns_3, mine, mask, q_rows, g_rows,
    keys_t0, expo_0, grad_prob_0, stats_0, keys_t1, expo_1, grad_prob_1, stats_1,
    keys_t2, expo_2, grad_prob_2, stats_2,
    query_grad, own_key_grad, own_value_grad, prompt_grads,
    key_rows, value_rows, keys_t3, expo_3, grad_prob_3, stats_3, scores, grad_score, key_acc, value_acc, dq_t,
):
    columns = (columns_0, columns_1, columns_2, columns_3)
    along_x, along_z = len(columns), columns_0.shape[0]
    block = columns_0.shape[1] - META
    half = block // 2
    width = q_rows.shape[0]
    comp_len = mask.shape[1]
    members = along_x * along_z

    length_sum = jnp.zeros((1, 128), jnp.float32)
    reward_sum = jnp.zeros((1, 128), jnp.float32)
    square_sum = jnp.zeros((1, 128), jnp.float32)
    for column in columns:
        for i in range(along_z):
            meta = column[i, block:block + META, :].astype(jnp.float32)
            reward = meta[1:2, :]
            length_sum += meta[0:1, :]
            reward_sum += reward
            square_sum += reward * reward
    own_meta = mine[block:block + META, :].astype(jnp.float32)
    reward_mean = reward_sum / members
    variance = square_sum / members - reward_mean * reward_mean
    advantage = (own_meta[1:2, :] - reward_mean) / jnp.sqrt(variance + 1.0)
    positions = lax.broadcasted_iota(jnp.int32, (1, comp_len), 1).astype(jnp.float32)
    valid = jnp.where(positions < own_meta[0:1, :], mask[...].astype(jnp.float32), 0.0)
    weights = advantage * valid * (members * comp_len / length_sum)
    weight_row = jnp.concatenate([weights] * (TILE // comp_len), axis=1)

    copy_column(columns[3], key_rows, value_rows, 0)
    transpose_rows(key_rows, keys_t3)
    groups = (
        (keys_t0, expo_0, grad_prob_0, stats_0),
        (keys_t1, expo_1, grad_prob_1, stats_1),
        (keys_t2, expo_2, grad_prob_2, stats_2),
        (keys_t3, expo_3, grad_prob_3, stats_3),
    )
    for cols in tiles_of(width):
        forward_tile(
            cols, key_rows, value_rows, q_rows[cols, :], g_rows[cols, :],
            scores, expo_3, grad_prob_3, stats_3, 0, 0,
        )
    for j, cols in enumerate(tiles_of(width)):
        q_tile = q_rows[cols, :]
        g_tile = g_rows[cols, :]
        tops = [stats[0:1, cols] for *_, stats in groups]
        top = jnp.maximum(jnp.maximum(tops[0], tops[1]), jnp.maximum(tops[2], tops[3]))
        shares = [jnp.exp2((t - top) * (SCALE * LOG2E)) for t in tops]
        sums = sum(share * stats[8:16, cols] for share, (*_, stats) in zip(shares, groups))
        dots = sum(share * stats[16:24, cols] for share, (*_, stats) in zip(shares, groups))
        inverse = 1.0 / jnp.sum(sums, axis=0, keepdims=True)
        delta = jnp.sum(dots, axis=0, keepdims=True) * inverse
        factor = weight_row * inverse
        dq = None
        start = 0
        for share, (keys_t, expo, grad_prob, _) in zip(shares, groups):
            part = factor * share
            column = jnp.concatenate(
                [jnp.broadcast_to(part[:, k:k + 128], (128, 128)).T for k in range(0, TILE, 128)], axis=0
            )
            g_scaled = (g_tile.astype(jnp.float32) * column).astype(jnp.bfloat16)
            q_scaled = (q_tile.astype(jnp.float32) * (column * SCALE)).astype(jnp.bfloat16)
            total = keys_t.shape[1]
            chunk = 512 if total % 512 == 0 else total // 2
            for i in range(0, total, chunk):
                rows = slice(i, i + chunk)
                out = slice(start + i, start + i + chunk)
                e = expo[rows, cols]
                ds = (e.astype(jnp.float32) * (grad_prob[rows, cols] - delta)).astype(jnp.bfloat16)
                grad_score[out, :] = ds
                dv = jnp.dot(e, g_scaled, preferred_element_type=jnp.float32)
                dk = jnp.dot(ds, q_scaled, preferred_element_type=jnp.float32)
                value_acc[out, :] = dv if j == 0 else value_acc[out, :] + dv
                key_acc[out, :] = dk if j == 0 else key_acc[out, :] + dk
            some = jnp.dot(keys_t[...], grad_score[start:start + total, :], preferred_element_type=jnp.float32)
            some = some * (part * SCALE)
            dq = some if dq is None else dq + some
            start += total
        dq_t[j] = dq

    for h in range(width // HEAD_DIM):
        j, k = divmod(h * HEAD_DIM, TILE)
        query_grad[:, h * HEAD_DIM:(h + 1) * HEAD_DIM] = dq_t[j, :, k:k + HEAD_DIM].T
    own_start = along_z * half
    own_len = own_key_grad.shape[0]
    own_key_grad[...] = key_acc[own_start:own_start + own_len, :]
    own_value_grad[...] = value_acc[own_start:own_start + own_len, :]
    starts = [0] + [own_start + own_len + k * own_start for k in range(along_x - 1)]
    for start, shift in zip(starts, SHIFTS):
        target = lax.rem(place[0] + (along_x - shift), along_x)
        for i in range(along_z):
            rows = slice(start + i * half, start + (i + 1) * half)
            prompt_grads[target, i, :half, :] = key_acc[rows, :].astype(jnp.bfloat16)
            prompt_grads[target, i, half:, :] = value_acc[rows, :].astype(jnp.bfloat16)


def forward_outputs(total, width):
    return (
        jax.ShapeDtypeStruct((HEAD_DIM, total), jnp.bfloat16),
        jax.ShapeDtypeStruct((total, width), jnp.bfloat16),
        jax.ShapeDtypeStruct((total, width), jnp.float32),
        jax.ShapeDtypeStruct((24, width), jnp.float32),
    )


def scratch(total):
    return [
        pltpu.VMEM((total, HEAD_DIM), jnp.bfloat16),
        pltpu.VMEM((total, HEAD_DIM), jnp.bfloat16),
    ]


VMEM = pl.BlockSpec(memory_space=pltpu.VMEM)


def params(mebibytes):
    return pltpu.CompilerParams(vmem_limit_bytes=mebibytes * 1024 * 1024)


def cost(total, width, passes):
    units = total * width
    return pl.CostEstimate(flops=2 * HEAD_DIM * units * passes, bytes_accessed=0, transcendentals=units)


def own_forward(column, own_key, own_value, queries, grads):
    width = queries.shape[1]
    total = column.shape[0] * (column.shape[1] - META) // 2 + own_key.shape[0]
    rows = jax.ShapeDtypeStruct((width, HEAD_DIM), jnp.bfloat16)
    outs = (rows, rows, *forward_outputs(total, width))
    return pl.pallas_call(
        own_kernel,
        out_shape=outs,
        in_specs=[VMEM] * 5,
        out_specs=(VMEM,) * len(outs),
        scratch_shapes=[*scratch(total), pltpu.VMEM((total, TILE), jnp.float32)],
        compiler_params=params(24),
        cost_estimate=cost(total, width, 2),
        name="own_forward",
    )(column, own_key, own_value, queries, grads)


def near_forward(column, q_rows, g_rows):
    width = q_rows.shape[0]
    total = column.shape[0] * (column.shape[1] - META) // 2
    outs = forward_outputs(total, width)
    return pl.pallas_call(
        near_kernel,
        out_shape=outs,
        in_specs=[VMEM] * 3,
        out_specs=(VMEM,) * len(outs),
        scratch_shapes=[*scratch(total), pltpu.VMEM((total, TILE), jnp.float32)],
        compiler_params=params(24),
        cost_estimate=cost(total, width, 2),
        name="near_forward",
    )(column, q_rows, g_rows)


def last_and_backward(place, columns, mine, mask, q_rows, g_rows, own_state, near_state):
    width = q_rows.shape[0]
    along_z, packed, dim = columns[0].shape
    block = packed - META
    comp_len = mask.shape[1]
    column_rows = along_z * block // 2
    own_len = own_state[0].shape[1] - column_rows
    total = len(columns) * column_rows + own_len
    f32, bf16 = jnp.float32, jnp.bfloat16
    state = [*own_state, *near_state]
    return pl.pallas_call(
        last_kernel,
        out_shape=(
            jax.ShapeDtypeStruct((comp_len, width), f32),
            jax.ShapeDtypeStruct((own_len, dim), f32),
            jax.ShapeDtypeStruct((own_len, dim), f32),
            jax.ShapeDtypeStruct((len(columns), along_z, block, dim), bf16),
        ),
        in_specs=[pl.BlockSpec(memory_space=pltpu.SMEM)] + [VMEM] * (len(columns) + 4 + len(state)),
        out_specs=(VMEM,) * 4,
        scratch_shapes=[
            *scratch(column_rows),
            *[pltpu.VMEM(out.shape, out.dtype) for out in forward_outputs(column_rows, width)],
            pltpu.VMEM((column_rows, TILE), f32),
            pltpu.VMEM((total, TILE), bf16),
            pltpu.VMEM((total, dim), f32),
            pltpu.VMEM((total, dim), f32),
            pltpu.VMEM((width // TILE, dim, TILE), f32),
        ],
        compiler_params=params(36),
        cost_estimate=cost(total, width, 4),
        name="last_and_backward",
    )(place, *columns, mine, mask, q_rows, g_rows, *state)


def shifted(column, shift):
    size = lax.axis_size("gx")
    return lax.ppermute(column, "gx", [(i, (i + shift) % size) for i in range(size)])


def body(queries, comp_keys, comp_values, prompt_keys, prompt_values, out_grad, lengths, loss_mask, buckets):
    row = lax.broadcasted_iota(jnp.int32, (META, prompt_keys.shape[1]), 0)
    meta = jnp.where(row == 0, lengths[0], jnp.where(row == 1, buckets[0], 0)).astype(jnp.bfloat16)
    mine = jnp.concatenate([prompt_keys, prompt_values, meta], axis=0)
    column = lax.all_gather(mine, "gz")
    columns = [column] + [None] * 3
    for k in (3, 1, 2):
        columns[k] = shifted(column, SHIFTS[k])
    q_rows, g_rows, *own_state = own_forward(column, comp_keys[0], comp_values[0], queries[0], out_grad[0])
    near_state = [*near_forward(columns[1], q_rows, g_rows), *near_forward(columns[2], q_rows, g_rows)]
    place = lax.axis_index("gx").astype(jnp.int32)[None]
    query_grad, own_key_grad, own_value_grad, prompt_grads = last_and_backward(
        place, columns, mine, loss_mask, q_rows, g_rows, own_state, near_state
    )
    terms = lax.all_to_all(prompt_grads, "gx", 0, 0)
    partial = jnp.sum(terms.astype(jnp.float32), axis=0).astype(jnp.bfloat16)
    terms = lax.all_to_all(jnp.stack([partial[i] for i in Z_ORDER]), "gz", 0, 0, axis_index_groups=[Z_ORDER])
    owned = jnp.sum(terms.astype(jnp.float32), axis=0)
    half = owned.shape[0] // 2
    return (
        query_grad[None],
        own_key_grad[None],
        own_value_grad[None],
        owned[:half],
        owned[half:],
    )


def solution(mesh):
    dp, group, tensor = (mesh.shape[name] for name in ("dp", "group", "tensor"))
    along_z = 4
    split = jax.sharding.Mesh(
        mesh.devices.reshape(dp, group // along_z, along_z, tensor), ("dp", "gx", "gz", "tensor")
    )
    rows = ("dp", "gx", "gz")
    return jax.shard_map(
        body,
        mesh=split,
        in_specs=(
            P(rows, None, "tensor"),
            P(rows, None, "tensor"),
            P(rows, None, "tensor"),
            P(rows, "tensor"),
            P(rows, "tensor"),
            P(rows, None, "tensor"),
            P(rows),
            P(rows, None),
            P(rows),
        ),
        out_specs=(
            P(rows, None, "tensor"),
            P(rows, None, "tensor"),
            P(rows, None, "tensor"),
            P(rows, "tensor"),
            P(rows, "tensor"),
        ),
        check_vma=False,
    )
```

```python
import jax
import jax.numpy as jnp
from jax import lax
from jax.experimental import pallas as pl
from jax.experimental.pallas import tpu as pltpu
from jax.sharding import PartitionSpec as P

HEAD_DIM = 128
SCALE = HEAD_DIM ** (-0.5)
LOG2E = 1.4426950408889634
META = 16
Z_ORDER = [2, 1, 0, 3]
SHIFTS = (0, 1, 3, 2)
TILE = 512
NT = (((1,), (1,)), ((), ()))


def fold_rows(values, op):
    rows, cols = values.shape
    return op(values.reshape(rows // 8, 8, cols), axis=0)


def copy_column(column, key_rows, value_rows, start):
    blocks, packed, _ = column.shape
    half = (packed - META) // 2
    for i in range(blocks):
        rows = slice(start + i * half, start + (i + 1) * half)
        key_rows[rows, :] = column[i, :half, :]
        value_rows[rows, :] = column[i, half:2 * half, :]


def transpose_rows(rows_ref, out):
    for i in range(0, rows_ref.shape[0], 128):
        out[:, i:i + 128] = rows_ref[i:i + 128, :].T


def forward_tile(cols, key_rows, value_rows, q_tile, g_tile, scores, expo, grad_prob, stats, own_len, comp_len):
    total = key_rows.shape[0]
    width = q_tile.shape[0]
    chunk = 512 if total % 512 == 0 else total // 2
    largest = jnp.full((8, width), -jnp.inf, jnp.float32)
    for i in range(0, total, chunk):
        rows = slice(i, i + chunk)
        s = lax.dot_general(key_rows[rows, :], q_tile, NT, preferred_element_type=jnp.float32)
        if own_len and i + chunk == total:
            own = s[chunk - own_len:, :]
            key_pos = lax.broadcasted_iota(jnp.int32, own.shape, 0)
            row_pos = lax.broadcasted_iota(jnp.int32, own.shape, 1) % comp_len
            own = jnp.where(key_pos <= row_pos, own, -jnp.inf)
            s = jnp.concatenate([s[:chunk - own_len, :], own], axis=0)
        scores[rows, :] = s
        largest = jnp.maximum(largest, fold_rows(s, jnp.max))
    top = jnp.max(largest, axis=0, keepdims=True)
    sums = jnp.zeros((8, width), jnp.float32)
    dots = jnp.zeros((8, width), jnp.float32)
    for i in range(0, total, chunk):
        rows = slice(i, i + chunk)
        dp = lax.dot_general(value_rows[rows, :], g_tile, NT, preferred_element_type=jnp.float32)
        e = jnp.exp2((scores[rows, :] - top) * (SCALE * LOG2E))
        expo[rows, cols] = e.astype(jnp.bfloat16)
        grad_prob[rows, cols] = dp
        sums += fold_rows(e, jnp.sum)
        dots += fold_rows(e * dp, jnp.sum)
    stats[0:8, cols] = jnp.broadcast_to(top, (8, width))
    stats[8:16, cols] = sums
    stats[16:24, cols] = dots


def tiles_of(width):
    return [slice(j, j + TILE) for j in range(0, width, TILE)]


def own_kernel(
    column, own_key, own_value, queries, grads,
    q_rows, g_rows, keys_t, expo, grad_prob, stats,
    key_rows, value_rows, scores,
):
    comp_len, width = queries.shape
    own_len = own_key.shape[0]
    for h in range(width // HEAD_DIM):
        q_rows[h * comp_len:(h + 1) * comp_len, :] = queries[:, h * HEAD_DIM:(h + 1) * HEAD_DIM]
        g_rows[h * comp_len:(h + 1) * comp_len, :] = grads[:, h * HEAD_DIM:(h + 1) * HEAD_DIM]
    copy_column(column, key_rows, value_rows, 0)
    start = key_rows.shape[0] - own_len
    key_rows[start:, :] = own_key[...]
    value_rows[start:, :] = own_value[...]
    transpose_rows(key_rows, keys_t)
    for cols in tiles_of(width):
        forward_tile(
            cols, key_rows, value_rows, q_rows[cols, :], g_rows[cols, :],
            scores, expo, grad_prob, stats, own_len, comp_len,
        )


def near_kernel(
    column, q_rows, g_rows,
    keys_t, expo, grad_prob, stats,
    key_rows, value_rows, scores,
):
    copy_column(column, key_rows, value_rows, 0)
    transpose_rows(key_rows, keys_t)
    for cols in tiles_of(q_rows.shape[0]):
        forward_tile(
            cols, key_rows, value_rows, q_rows[cols, :], g_rows[cols, :],
            scores, expo, grad_prob, stats, 0, 0,
        )


def last_kernel(
    place, columns_0, columns_1, columns_2, columns_3, mine, mask, q_rows, g_rows,
    keys_t0, expo_0, grad_prob_0, stats_0, keys_t1, expo_1, grad_prob_1, stats_1,
    keys_t2, expo_2, grad_prob_2, stats_2,
    query_grad, own_key_grad, own_value_grad, prompt_grads,
    key_rows, value_rows, keys_t3, expo_3, grad_prob_3, stats_3, scores, grad_score, key_acc, value_acc, dq_t,
):
    columns = (columns_0, columns_1, columns_2, columns_3)
    along_x, along_z = len(columns), columns_0.shape[0]
    block = columns_0.shape[1] - META
    half = block // 2
    width = q_rows.shape[0]
    comp_len = mask.shape[1]
    members = along_x * along_z

    length_sum = jnp.zeros((1, 128), jnp.float32)
    reward_sum = jnp.zeros((1, 128), jnp.float32)
    square_sum = jnp.zeros((1, 128), jnp.float32)
    for column in columns:
        for i in range(along_z):
            meta = column[i, block:block + META, :].astype(jnp.float32)
            reward = meta[1:2, :]
            length_sum += meta[0:1, :]
            reward_sum += reward
            square_sum += reward * reward
    own_meta = mine[block:block + META, :].astype(jnp.float32)
    reward_mean = reward_sum / members
    variance = square_sum / members - reward_mean * reward_mean
    advantage = (own_meta[1:2, :] - reward_mean) / jnp.sqrt(variance + 1.0)
    positions = lax.broadcasted_iota(jnp.int32, (1, comp_len), 1).astype(jnp.float32)
    valid = jnp.where(positions < own_meta[0:1, :], mask[...].astype(jnp.float32), 0.0)
    weights = advantage * valid * (members * comp_len / length_sum)
    weight_row = jnp.concatenate([weights] * (TILE // comp_len), axis=1)

    copy_column(columns[3], key_rows, value_rows, 0)
    transpose_rows(key_rows, keys_t3)
    groups = (
        (keys_t0, expo_0, grad_prob_0, stats_0),
        (keys_t1, expo_1, grad_prob_1, stats_1),
        (keys_t2, expo_2, grad_prob_2, stats_2),
        (keys_t3, expo_3, grad_prob_3, stats_3),
    )
    for cols in tiles_of(width):
        forward_tile(
            cols, key_rows, value_rows, q_rows[cols, :], g_rows[cols, :],
            scores, expo_3, grad_prob_3, stats_3, 0, 0,
        )
    for j, cols in enumerate(tiles_of(width)):
        q_tile = q_rows[cols, :]
        g_tile = g_rows[cols, :]
        tops = [stats[0:1, cols] for *_, stats in groups]
        top = jnp.maximum(jnp.maximum(tops[0], tops[1]), jnp.maximum(tops[2], tops[3]))
        shares = [jnp.exp2((t - top) * (SCALE * LOG2E)) for t in tops]
        sums = sum(share * stats[8:16, cols] for share, (*_, stats) in zip(shares, groups))
        dots = sum(share * stats[16:24, cols] for share, (*_, stats) in zip(shares, groups))
        inverse = 1.0 / jnp.sum(sums, axis=0, keepdims=True)
        delta = jnp.sum(dots, axis=0, keepdims=True) * inverse
        factor = weight_row * inverse
        dq = None
        start = 0
        for share, (keys_t, expo, grad_prob, _) in zip(shares, groups):
            part = factor * share
            column = jnp.concatenate(
                [jnp.broadcast_to(part[:, k:k + 128], (128, 128)).T for k in range(0, TILE, 128)], axis=0
            )
            g_scaled = (g_tile.astype(jnp.float32) * column).astype(jnp.bfloat16)
            q_scaled = (q_tile.astype(jnp.float32) * (column * SCALE)).astype(jnp.bfloat16)
            total = keys_t.shape[1]
            chunk = 512 if total % 512 == 0 else total // 2
            for i in range(0, total, chunk):
                rows = slice(i, i + chunk)
                out = slice(start + i, start + i + chunk)
                e = expo[rows, cols]
                ds = (e.astype(jnp.float32) * (grad_prob[rows, cols] - delta)).astype(jnp.bfloat16)
                grad_score[out, :] = ds
                dv = jnp.dot(e, g_scaled, preferred_element_type=jnp.float32)
                dk = jnp.dot(ds, q_scaled, preferred_element_type=jnp.float32)
                value_acc[out, :] = dv if j == 0 else value_acc[out, :] + dv
                key_acc[out, :] = dk if j == 0 else key_acc[out, :] + dk
            some = jnp.dot(keys_t[...], grad_score[start:start + total, :], preferred_element_type=jnp.float32)
            some = some * (part * SCALE)
            dq = some if dq is None else dq + some
            start += total
        dq_t[j] = dq

    for h in range(width // HEAD_DIM):
        j, k = divmod(h * HEAD_DIM, TILE)
        query_grad[:, h * HEAD_DIM:(h + 1) * HEAD_DIM] = dq_t[j, :, k:k + HEAD_DIM].T
    own_start = along_z * half
    own_len = own_key_grad.shape[0]
    own_key_grad[...] = key_acc[own_start:own_start + own_len, :]
    own_value_grad[...] = value_acc[own_start:own_start + own_len, :]
    starts = [0] + [own_start + own_len + k * own_start for k in range(along_x - 1)]
    for start, shift in zip(starts, SHIFTS):
        target = lax.rem(place[0] + (along_x - shift), along_x)
        for i in range(along_z):
            rows = slice(start + i * half, start + (i + 1) * half)
            prompt_grads[target, i, :half, :] = key_acc[rows, :].astype(jnp.bfloat16)
            prompt_grads[target, i, half:, :] = value_acc[rows, :].astype(jnp.bfloat16)


def forward_outputs(total, width):
    return (
        jax.ShapeDtypeStruct((HEAD_DIM, total), jnp.bfloat16),
        jax.ShapeDtypeStruct((total, width), jnp.bfloat16),
        jax.ShapeDtypeStruct((total, width), jnp.float32),
        jax.ShapeDtypeStruct((24, width), jnp.float32),
    )


def scratch(total):
    return [
        pltpu.VMEM((total, HEAD_DIM), jnp.bfloat16),
        pltpu.VMEM((total, HEAD_DIM), jnp.bfloat16),
    ]


VMEM = pl.BlockSpec(memory_space=pltpu.VMEM)


def params(mebibytes):
    return pltpu.CompilerParams(vmem_limit_bytes=mebibytes * 1024 * 1024)


def cost(total, width, passes):
    units = total * width
    return pl.CostEstimate(flops=2 * HEAD_DIM * units * passes, bytes_accessed=0, transcendentals=units)


def own_forward(column, own_key, own_value, queries, grads):
    width = queries.shape[1]
    total = column.shape[0] * (column.shape[1] - META) // 2 + own_key.shape[0]
    rows = jax.ShapeDtypeStruct((width, HEAD_DIM), jnp.bfloat16)
    outs = (rows, rows, *forward_outputs(total, width))
    return pl.pallas_call(
        own_kernel,
        out_shape=outs,
        in_specs=[VMEM] * 5,
        out_specs=(VMEM,) * len(outs),
        scratch_shapes=[*scratch(total), pltpu.VMEM((total, TILE), jnp.float32)],
        compiler_params=params(24),
        cost_estimate=cost(total, width, 2),
        name="own_forward",
    )(column, own_key, own_value, queries, grads)


def near_forward(column, q_rows, g_rows):
    width = q_rows.shape[0]
    total = column.shape[0] * (column.shape[1] - META) // 2
    outs = forward_outputs(total, width)
    return pl.pallas_call(
        near_kernel,
        out_shape=outs,
        in_specs=[VMEM] * 3,
        out_specs=(VMEM,) * len(outs),
        scratch_shapes=[*scratch(total), pltpu.VMEM((total, TILE), jnp.float32)],
        compiler_params=params(24),
        cost_estimate=cost(total, width, 2),
        name="near_forward",
    )(column, q_rows, g_rows)


def last_and_backward(place, columns, mine, mask, q_rows, g_rows, own_state, near_state):
    width = q_rows.shape[0]
    along_z, packed, dim = columns[0].shape
    block = packed - META
    comp_len = mask.shape[1]
    column_rows = along_z * block // 2
    own_len = own_state[0].shape[1] - column_rows
    total = len(columns) * column_rows + own_len
    f32, bf16 = jnp.float32, jnp.bfloat16
    state = [*own_state, *near_state]
    return pl.pallas_call(
        last_kernel,
        out_shape=(
            jax.ShapeDtypeStruct((comp_len, width), f32),
            jax.ShapeDtypeStruct((own_len, dim), f32),
            jax.ShapeDtypeStruct((own_len, dim), f32),
            jax.ShapeDtypeStruct((len(columns), along_z, block, dim), bf16),
        ),
        in_specs=[pl.BlockSpec(memory_space=pltpu.SMEM)] + [VMEM] * (len(columns) + 4 + len(state)),
        out_specs=(VMEM,) * 4,
        scratch_shapes=[
            *scratch(column_rows),
            *[pltpu.VMEM(out.shape, out.dtype) for out in forward_outputs(column_rows, width)],
            pltpu.VMEM((column_rows, TILE), f32),
            pltpu.VMEM((total, TILE), bf16),
            pltpu.VMEM((total, dim), f32),
            pltpu.VMEM((total, dim), f32),
            pltpu.VMEM((width // TILE, dim, TILE), f32),
        ],
        compiler_params=params(36),
        cost_estimate=cost(total, width, 4),
        name="last_and_backward",
    )(place, *columns, mine, mask, q_rows, g_rows, *state)


def shifted(column, shift):
    size = lax.axis_size("gx")
    return lax.ppermute(column, "gx", [(i, (i + shift) % size) for i in range(size)])


def body(queries, comp_keys, comp_values, prompt_keys, prompt_values, out_grad, lengths, loss_mask, buckets):
    row = lax.broadcasted_iota(jnp.int32, (META, prompt_keys.shape[1]), 0)
    meta = jnp.where(row == 0, lengths[0], jnp.where(row == 1, buckets[0], 0)).astype(jnp.bfloat16)
    mine = jnp.concatenate([prompt_keys, prompt_values, meta], axis=0)
    column = lax.all_gather(mine, "gz")
    columns = [column] + [None] * 3
    for k in (3, 1, 2):
        columns[k] = shifted(column, SHIFTS[k])
    q_rows, g_rows, *own_state = own_forward(column, comp_keys[0], comp_values[0], queries[0], out_grad[0])
    near_state = [*near_forward(columns[1], q_rows, g_rows), *near_forward(columns[2], q_rows, g_rows)]
    place = lax.axis_index("gx").astype(jnp.int32)[None]
    query_grad, own_key_grad, own_value_grad, prompt_grads = last_and_backward(
        place, columns, mine, loss_mask, q_rows, g_rows, own_state, near_state
    )
    terms = lax.all_to_all(prompt_grads, "gx", 0, 0)
    partial = jnp.sum(terms.astype(jnp.float32), axis=0).astype(jnp.bfloat16)
    terms = lax.all_to_all(jnp.stack([partial[i] for i in Z_ORDER]), "gz", 0, 0, axis_index_groups=[Z_ORDER])
    half = terms.shape[1] // 2
    owned_keys = jnp.sum(terms[:, :half].astype(jnp.float32), axis=0)
    owned_values = jnp.sum(terms[:, half:].astype(jnp.float32), axis=0)
    return (
        query_grad[None],
        own_key_grad[None],
        own_value_grad[None],
        owned_keys,
        owned_values,
    )


def solution(mesh):
    dp, group, tensor = (mesh.shape[name] for name in ("dp", "group", "tensor"))
    along_z = 4
    split = jax.sharding.Mesh(
        mesh.devices.reshape(dp, group // along_z, along_z, tensor), ("dp", "gx", "gz", "tensor")
    )
    rows = ("dp", "gx", "gz")
    return jax.shard_map(
        body,
        mesh=split,
        in_specs=(
            P(rows, None, "tensor"),
            P(rows, None, "tensor"),
            P(rows, None, "tensor"),
            P(rows, "tensor"),
            P(rows, "tensor"),
            P(rows, None, "tensor"),
            P(rows),
            P(rows, None),
            P(rows),
        ),
        out_specs=(
            P(rows, None, "tensor"),
            P(rows, None, "tensor"),
            P(rows, None, "tensor"),
            P(rows, "tensor"),
            P(rows, "tensor"),
        ),
        check_vma=False,
    )
```

```python
import jax
import jax.numpy as jnp
from jax import lax
from jax.experimental import pallas as pl
from jax.experimental.pallas import tpu as pltpu
from jax.sharding import PartitionSpec as P

HEAD_DIM = 128
SCALE = HEAD_DIM ** (-0.5)
LOG2E = 1.4426950408889634
META = 16
Z_ORDER = [2, 3, 0, 1]
SHIFTS = (0, 1, 3, 2)
TILE = 512
NT = (((1,), (1,)), ((), ()))


def fold_rows(values, op):
    rows, cols = values.shape
    return op(values.reshape(rows // 8, 8, cols), axis=0)


def copy_column(column, key_rows, value_rows, start):
    blocks, packed, _ = column.shape
    half = (packed - META) // 2
    for i in range(blocks):
        rows = slice(start + i * half, start + (i + 1) * half)
        key_rows[rows, :] = column[i, :half, :]
        value_rows[rows, :] = column[i, half:2 * half, :]


def transpose_rows(rows_ref, out):
    for i in range(0, rows_ref.shape[0], 128):
        out[:, i:i + 128] = rows_ref[i:i + 128, :].T


def forward_tile(cols, key_rows, value_rows, q_tile, g_tile, scores, expo, grad_prob, stats, own_len, comp_len):
    total = key_rows.shape[0]
    width = q_tile.shape[0]
    chunk = 512 if total % 512 == 0 else total // 2
    largest = jnp.full((8, width), -jnp.inf, jnp.float32)
    for i in range(0, total, chunk):
        rows = slice(i, i + chunk)
        s = lax.dot_general(key_rows[rows, :], q_tile, NT, preferred_element_type=jnp.float32)
        if own_len and i + chunk == total:
            own = s[chunk - own_len:, :]
            key_pos = lax.broadcasted_iota(jnp.int32, own.shape, 0)
            row_pos = lax.broadcasted_iota(jnp.int32, own.shape, 1) % comp_len
            own = jnp.where(key_pos <= row_pos, own, -jnp.inf)
            s = jnp.concatenate([s[:chunk - own_len, :], own], axis=0)
        scores[rows, :] = s
        largest = jnp.maximum(largest, fold_rows(s, jnp.max))
    top = jnp.max(largest, axis=0, keepdims=True)
    sums = jnp.zeros((8, width), jnp.float32)
    dots = jnp.zeros((8, width), jnp.float32)
    for i in range(0, total, chunk):
        rows = slice(i, i + chunk)
        dp = lax.dot_general(value_rows[rows, :], g_tile, NT, preferred_element_type=jnp.float32)
        e = jnp.exp2((scores[rows, :] - top) * (SCALE * LOG2E))
        expo[rows, cols] = e.astype(jnp.bfloat16)
        grad_prob[rows, cols] = dp
        sums += fold_rows(e, jnp.sum)
        dots += fold_rows(e * dp, jnp.sum)
    stats[0:8, cols] = jnp.broadcast_to(top, (8, width))
    stats[8:16, cols] = sums
    stats[16:24, cols] = dots


def tiles_of(width):
    return [slice(j, j + TILE) for j in range(0, width, TILE)]


def own_kernel(
    column, own_key, own_value, queries, grads,
    q_rows, g_rows, keys_t, expo, grad_prob, stats,
    key_rows, value_rows, scores,
):
    comp_len, width = queries.shape
    own_len = own_key.shape[0]
    for h in range(width // HEAD_DIM):
        q_rows[h * comp_len:(h + 1) * comp_len, :] = queries[:, h * HEAD_DIM:(h + 1) * HEAD_DIM]
        g_rows[h * comp_len:(h + 1) * comp_len, :] = grads[:, h * HEAD_DIM:(h + 1) * HEAD_DIM]
    copy_column(column, key_rows, value_rows, 0)
    start = key_rows.shape[0] - own_len
    key_rows[start:, :] = own_key[...]
    value_rows[start:, :] = own_value[...]
    transpose_rows(key_rows, keys_t)
    for cols in tiles_of(width):
        forward_tile(
            cols, key_rows, value_rows, q_rows[cols, :], g_rows[cols, :],
            scores, expo, grad_prob, stats, own_len, comp_len,
        )


def near_kernel(
    column, q_rows, g_rows,
    keys_t, expo, grad_prob, stats,
    key_rows, value_rows, scores,
):
    copy_column(column, key_rows, value_rows, 0)
    transpose_rows(key_rows, keys_t)
    for cols in tiles_of(q_rows.shape[0]):
        forward_tile(
            cols, key_rows, value_rows, q_rows[cols, :], g_rows[cols, :],
            scores, expo, grad_prob, stats, 0, 0,
        )


def last_kernel(
    place, columns_0, columns_1, columns_2, columns_3, mine, mask, q_rows, g_rows,
    keys_t0, expo_0, grad_prob_0, stats_0, keys_t1, expo_1, grad_prob_1, stats_1,
    keys_t2, expo_2, grad_prob_2, stats_2,
    query_grad, own_key_grad, own_value_grad, prompt_grads,
    key_rows, value_rows, keys_t3, expo_3, grad_prob_3, stats_3, scores, grad_score, key_acc, value_acc, dq_t,
):
    columns = (columns_0, columns_1, columns_2, columns_3)
    along_x, along_z = len(columns), columns_0.shape[0]
    block = columns_0.shape[1] - META
    half = block // 2
    width = q_rows.shape[0]
    comp_len = mask.shape[1]
    members = along_x * along_z

    length_sum = jnp.zeros((1, 128), jnp.float32)
    reward_sum = jnp.zeros((1, 128), jnp.float32)
    square_sum = jnp.zeros((1, 128), jnp.float32)
    for column in columns:
        for i in range(along_z):
            meta = column[i, block:block + META, :].astype(jnp.float32)
            reward = meta[1:2, :]
            length_sum += meta[0:1, :]
            reward_sum += reward
            square_sum += reward * reward
    own_meta = mine[block:block + META, :].astype(jnp.float32)
    reward_mean = reward_sum / members
    variance = square_sum / members - reward_mean * reward_mean
    advantage = (own_meta[1:2, :] - reward_mean) / jnp.sqrt(variance + 1.0)
    positions = lax.broadcasted_iota(jnp.int32, (1, comp_len), 1).astype(jnp.float32)
    valid = jnp.where(positions < own_meta[0:1, :], mask[...].astype(jnp.float32), 0.0)
    weights = advantage * valid * (members * comp_len / length_sum)
    weight_row = jnp.concatenate([weights] * (TILE // comp_len), axis=1)

    copy_column(columns[3], key_rows, value_rows, 0)
    transpose_rows(key_rows, keys_t3)
    groups = (
        (keys_t0, expo_0, grad_prob_0, stats_0),
        (keys_t1, expo_1, grad_prob_1, stats_1),
        (keys_t2, expo_2, grad_prob_2, stats_2),
        (keys_t3, expo_3, grad_prob_3, stats_3),
    )
    for cols in tiles_of(width):
        forward_tile(
            cols, key_rows, value_rows, q_rows[cols, :], g_rows[cols, :],
            scores, expo_3, grad_prob_3, stats_3, 0, 0,
        )
    for j, cols in enumerate(tiles_of(width)):
        q_tile = q_rows[cols, :]
        g_tile = g_rows[cols, :]
        tops = [stats[0:1, cols] for *_, stats in groups]
        top = jnp.maximum(jnp.maximum(tops[0], tops[1]), jnp.maximum(tops[2], tops[3]))
        shares = [jnp.exp2((t - top) * (SCALE * LOG2E)) for t in tops]
        sums = sum(share * stats[8:16, cols] for share, (*_, stats) in zip(shares, groups))
        dots = sum(share * stats[16:24, cols] for share, (*_, stats) in zip(shares, groups))
        inverse = 1.0 / jnp.sum(sums, axis=0, keepdims=True)
        delta = jnp.sum(dots, axis=0, keepdims=True) * inverse
        factor = weight_row * inverse
        dq = None
        start = 0
        for share, (keys_t, expo, grad_prob, _) in zip(shares, groups):
            part = factor * share
            column = jnp.concatenate(
                [jnp.broadcast_to(part[:, k:k + 128], (128, 128)).T for k in range(0, TILE, 128)], axis=0
            )
            g_scaled = (g_tile.astype(jnp.float32) * column).astype(jnp.bfloat16)
            q_scaled = (q_tile.astype(jnp.float32) * (column * SCALE)).astype(jnp.bfloat16)
            total = keys_t.shape[1]
            chunk = 512 if total % 512 == 0 else total // 2
            for i in range(0, total, chunk):
                rows = slice(i, i + chunk)
                out = slice(start + i, start + i + chunk)
                e = expo[rows, cols]
                ds = (e.astype(jnp.float32) * (grad_prob[rows, cols] - delta)).astype(jnp.bfloat16)
                grad_score[out, :] = ds
                dv = jnp.dot(e, g_scaled, preferred_element_type=jnp.float32)
                dk = jnp.dot(ds, q_scaled, preferred_element_type=jnp.float32)
                value_acc[out, :] = dv if j == 0 else value_acc[out, :] + dv
                key_acc[out, :] = dk if j == 0 else key_acc[out, :] + dk
            some = jnp.dot(keys_t[...], grad_score[start:start + total, :], preferred_element_type=jnp.float32)
            some = some * (part * SCALE)
            dq = some if dq is None else dq + some
            start += total
        dq_t[j] = dq

    for h in range(width // HEAD_DIM):
        j, k = divmod(h * HEAD_DIM, TILE)
        query_grad[:, h * HEAD_DIM:(h + 1) * HEAD_DIM] = dq_t[j, :, k:k + HEAD_DIM].T
    own_start = along_z * half
    own_len = own_key_grad.shape[0]
    own_key_grad[...] = key_acc[own_start:own_start + own_len, :]
    own_value_grad[...] = value_acc[own_start:own_start + own_len, :]
    starts = [0] + [own_start + own_len + k * own_start for k in range(along_x - 1)]
    for start, shift in zip(starts, SHIFTS):
        target = lax.rem(place[0] + (along_x - shift), along_x)
        for i in range(along_z):
            rows = slice(start + i * half, start + (i + 1) * half)
            prompt_grads[target, i, :half, :] = key_acc[rows, :].astype(jnp.bfloat16)
            prompt_grads[target, i, half:, :] = value_acc[rows, :].astype(jnp.bfloat16)


def forward_outputs(total, width):
    return (
        jax.ShapeDtypeStruct((HEAD_DIM, total), jnp.bfloat16),
        jax.ShapeDtypeStruct((total, width), jnp.bfloat16),
        jax.ShapeDtypeStruct((total, width), jnp.float32),
        jax.ShapeDtypeStruct((24, width), jnp.float32),
    )


def scratch(total):
    return [
        pltpu.VMEM((total, HEAD_DIM), jnp.bfloat16),
        pltpu.VMEM((total, HEAD_DIM), jnp.bfloat16),
    ]


VMEM = pl.BlockSpec(memory_space=pltpu.VMEM)


def params(mebibytes):
    return pltpu.CompilerParams(vmem_limit_bytes=mebibytes * 1024 * 1024)


def cost(total, width, passes):
    units = total * width
    return pl.CostEstimate(flops=2 * HEAD_DIM * units * passes, bytes_accessed=0, transcendentals=units)


def own_forward(column, own_key, own_value, queries, grads):
    width = queries.shape[1]
    total = column.shape[0] * (column.shape[1] - META) // 2 + own_key.shape[0]
    rows = jax.ShapeDtypeStruct((width, HEAD_DIM), jnp.bfloat16)
    outs = (rows, rows, *forward_outputs(total, width))
    return pl.pallas_call(
        own_kernel,
        out_shape=outs,
        in_specs=[VMEM] * 5,
        out_specs=(VMEM,) * len(outs),
        scratch_shapes=[*scratch(total), pltpu.VMEM((total, TILE), jnp.float32)],
        compiler_params=params(24),
        cost_estimate=cost(total, width, 2),
        name="own_forward",
    )(column, own_key, own_value, queries, grads)


def near_forward(column, q_rows, g_rows):
    width = q_rows.shape[0]
    total = column.shape[0] * (column.shape[1] - META) // 2
    outs = forward_outputs(total, width)
    return pl.pallas_call(
        near_kernel,
        out_shape=outs,
        in_specs=[VMEM] * 3,
        out_specs=(VMEM,) * len(outs),
        scratch_shapes=[*scratch(total), pltpu.VMEM((total, TILE), jnp.float32)],
        compiler_params=params(24),
        cost_estimate=cost(total, width, 2),
        name="near_forward",
    )(column, q_rows, g_rows)


def last_and_backward(place, columns, mine, mask, q_rows, g_rows, own_state, near_state):
    width = q_rows.shape[0]
    along_z, packed, dim = columns[0].shape
    block = packed - META
    comp_len = mask.shape[1]
    column_rows = along_z * block // 2
    own_len = own_state[0].shape[1] - column_rows
    total = len(columns) * column_rows + own_len
    f32, bf16 = jnp.float32, jnp.bfloat16
    state = [*own_state, *near_state]
    return pl.pallas_call(
        last_kernel,
        out_shape=(
            jax.ShapeDtypeStruct((comp_len, width), f32),
            jax.ShapeDtypeStruct((own_len, dim), f32),
            jax.ShapeDtypeStruct((own_len, dim), f32),
            jax.ShapeDtypeStruct((len(columns), along_z, block, dim), bf16),
        ),
        in_specs=[pl.BlockSpec(memory_space=pltpu.SMEM)] + [VMEM] * (len(columns) + 4 + len(state)),
        out_specs=(VMEM,) * 4,
        scratch_shapes=[
            *scratch(column_rows),
            *[pltpu.VMEM(out.shape, out.dtype) for out in forward_outputs(column_rows, width)],
            pltpu.VMEM((column_rows, TILE), f32),
            pltpu.VMEM((total, TILE), bf16),
            pltpu.VMEM((total, dim), f32),
            pltpu.VMEM((total, dim), f32),
            pltpu.VMEM((width // TILE, dim, TILE), f32),
        ],
        compiler_params=params(36),
        cost_estimate=cost(total, width, 4),
        name="last_and_backward",
    )(place, *columns, mine, mask, q_rows, g_rows, *state)


def shifted(column, shift):
    size = lax.axis_size("gx")
    return lax.ppermute(column, "gx", [(i, (i + shift) % size) for i in range(size)])


def body(queries, comp_keys, comp_values, prompt_keys, prompt_values, out_grad, lengths, loss_mask, buckets):
    row = lax.broadcasted_iota(jnp.int32, (META, prompt_keys.shape[1]), 0)
    meta = jnp.where(row == 0, lengths[0], jnp.where(row == 1, buckets[0], 0)).astype(jnp.bfloat16)
    mine = jnp.concatenate([prompt_keys, prompt_values, meta], axis=0)
    column = lax.all_gather(mine, "gz")
    columns = [column] + [None] * 3
    for k in (3, 1, 2):
        columns[k] = shifted(column, SHIFTS[k])
    q_rows, g_rows, *own_state = own_forward(column, comp_keys[0], comp_values[0], queries[0], out_grad[0])
    near_state = [*near_forward(columns[1], q_rows, g_rows), *near_forward(columns[2], q_rows, g_rows)]
    place = lax.axis_index("gx").astype(jnp.int32)[None]
    query_grad, own_key_grad, own_value_grad, prompt_grads = last_and_backward(
        place, columns, mine, loss_mask, q_rows, g_rows, own_state, near_state
    )
    terms = lax.all_to_all(prompt_grads, "gx", 0, 0)
    partial = jnp.sum(terms.astype(jnp.float32), axis=0).astype(jnp.bfloat16)
    terms = lax.all_to_all(jnp.stack([partial[i] for i in Z_ORDER]), "gz", 0, 0, axis_index_groups=[Z_ORDER])
    owned = jnp.sum(terms.astype(jnp.float32), axis=0)
    half = owned.shape[0] // 2
    return (
        query_grad[None],
        own_key_grad[None],
        own_value_grad[None],
        owned[:half],
        owned[half:],
    )


def solution(mesh):
    dp, group, tensor = (mesh.shape[name] for name in ("dp", "group", "tensor"))
    along_z = 4
    split = jax.sharding.Mesh(
        mesh.devices.reshape(dp, group // along_z, along_z, tensor), ("dp", "gx", "gz", "tensor")
    )
    rows = ("dp", "gx", "gz")
    return jax.shard_map(
        body,
        mesh=split,
        in_specs=(
            P(rows, None, "tensor"),
            P(rows, None, "tensor"),
            P(rows, None, "tensor"),
            P(rows, "tensor"),
            P(rows, "tensor"),
            P(rows, None, "tensor"),
            P(rows),
            P(rows, None),
            P(rows),
        ),
        out_specs=(
            P(rows, None, "tensor"),
            P(rows, None, "tensor"),
            P(rows, None, "tensor"),
            P(rows, "tensor"),
            P(rows, "tensor"),
        ),
        check_vma=False,
    )
```
